32 devices in a mesh: gx: 8 (over z, x), gy: 4 (over y, core).
Axes of the slice: x: 2, y: 2, z: 4, core: 2. Of those that a mesh axis runs over, the one named last changes fastest.
Arguments:
- rhs: float32 [48, 32, 192], P('gx', 'gy'), may hold values from -6 to 6
- diag_blocks: float32 [48, 32, 192, 192], P('gx', 'gy'), as said below
- east_blocks: float32 [48, 32, 192, 192], P('gx', 'gy')
- north_blocks: float32 [48, 32, 192, 192], P('gx', 'gy')
- face_open: int32 [48, 32, 2], P('gx', 'gy'), may hold values 0 or 1
- modes: float32 [48, 32, 6, 192], P('gx', 'gy'), may hold values from -0.21875 to 0.21875
- aggregate: int32 [48, 32], P('gx', 'gy'), may hold values from 0 to 15, as said below
- live_count: int32 [8, 4], P('gx', 'gy'), may hold values from 8 to 16, as said below
Outputs:
- smoothed: float32 [48, 32, 192], P('gx', 'gy')
- coarse_rows: float32 [8, 4, 64, 6, 288], P('gx', 'gy')
- coarse_rhs: float32 [8, 4, 64, 6], P('gx', 'gy')
The draws below stay inside these ranges and needn't reach their ends.
Inputs may be any that keep to these rules, and one draw needn't show every extreme that they name: `live_count`: some device has exactly 16 aggregates in use in every draw. `aggregate`: each element's slot is below its device's live_count. diag_blocks are symmetric.
All inputs are finite; a program needn't handle non-finite values. No bound on the sum of `face_open` on one device may be relied on, other than what follows from the above.
Results may differ from the reference program's by a relative error of at most 0.0003.
Values sent between devices are 32-bit elements; how exact they have to be, the bound alone decides.
A program may use at most 384 MiB of HBM per device.

```python
import math
import jax
import jax.numpy as jnp
from jax import lax

NB = 192
MODES = 6
CHEB = 4
EX = 6
EY = 8
AGG_DEV = 16
NX = 48
NY = 32
CAP = 64
COLS = 288


def coupling_scale(key, lowest, highest):
    key = jax.random.fold_in(key, 91)
    first, second = jax.random.split(key)
    strength = jnp.exp(jax.random.uniform(first, (), jnp.float32, math.log(lowest), math.log(highest)))
    ramp = 0.4 + 0.6 * jnp.arange(NX, dtype=jnp.float32) / NX
    rough = jnp.exp(jax.random.uniform(second, (NX, NY), jnp.float32, -0.22, 0.22))
    return strength * ramp[:, None] * rough


def live_counts(key):
    key = jax.random.fold_in(key, 57)
    first, second = jax.random.split(key)
    groups = NX // EX
    members = NY // EY
    counts = jax.random.randint(first, (groups, members), max(1, AGG_DEV // 2), AGG_DEV + 1)
    chosen = jax.random.randint(second, (), 0, groups * members)
    counts = counts.reshape(-1).at[chosen].set(AGG_DEV).reshape(groups, members)
    return (counts, chosen)


def draw_diag_blocks(key, part):
    scale = coupling_scale(key, 0.035, 0.05)
    key = jax.random.fold_in(key, 1)
    first, second = jax.random.split(key)
    noise = jax.random.normal(first, (NX, NY, NB, NB), jnp.float32)
    noise = noise * scale[:, :, None, None]
    symmetric = 0.5 * (noise + jnp.swapaxes(noise, 2, 3))
    main = jax.random.uniform(second, (NX, NY, NB), jnp.float32, 4.5, 7.0)
    return symmetric + main[..., None] * jnp.eye(NB, dtype=jnp.float32)


def draw_east_blocks(key, part):
    scale = coupling_scale(key, 0.035, 0.05)
    key = jax.random.fold_in(key, 2)
    noise = jax.random.normal(key, (NX, NY, NB, NB), jnp.float32)
    return noise * scale[:, :, None, None]


def draw_north_blocks(key, part):
    scale = coupling_scale(key, 0.035, 0.05)
    key = jax.random.fold_in(key, 3)
    noise = jax.random.normal(key, (NX, NY, NB, NB), jnp.float32)
    return noise * scale[:, :, None, None]


def draw_live_count(key, part):
    counts, chosen = live_counts(key)
    return counts


def draw_aggregate(key, part):
    counts, chosen = live_counts(key)
    key = jax.random.fold_in(key, 6)
    members = NY // EY
    spread = jnp.repeat(jnp.repeat(counts, EX, axis=0), EY, axis=1)
    slots = jax.random.randint(key, (NX, NY), 0, spread)
    row = chosen // members * EX
    column = chosen % members * EY
    return slots.at[row, column].set(AGG_DEV - 1)


def with_ends(entries, own_key, least, largest):
    dims = entries.shape
    index_at = [jax.random.randint(jax.random.fold_in(own_key, axis), (), 0, dims[axis]) for axis in range(len(dims))]
    entries = entries.at[tuple(index_at)].set(least)
    longest = dims.index(max(dims))
    index_at[longest] = (index_at[longest] + 1) % dims[longest]
    return entries.at[tuple(index_at)].set(largest)


def block_scale(key, shape, pieces, low, high):
    factor_of = 1.0
    for dim, parts in pieces:
        draws = jax.random.uniform(jax.random.fold_in(jax.random.fold_in(key, 6), dim), (parts,), jnp.float32, low / len(pieces), high / len(pieces))
        factor_of = factor_of * jnp.repeat(jnp.exp(draws), shape[dim] // parts).reshape((-1,) + (1,) * (len(shape) - 1 - dim))
    return factor_of


def scatter_about(stream_key, shape, deviation, bound, shards=(), held_as=jnp.bfloat16):
    drawn = jax.random.normal(stream_key, shape, jnp.float32) * deviation
    if len(shards) > 0:
        drawn = block_scale(stream_key, shape, shards, -0.22, 0.18) * drawn
    return jnp.clip(drawn, min=-bound, max=bound).astype(held_as)


def setup_inputs(seed: int = 0) -> dict:
    keys = jax.random.split(jax.random.key(seed), 9)
    return {
        "rhs": scatter_about(keys[0], (NX, NY, NB), 1.0, 6.0, ((0, 8), (1, 4)), jnp.float32),
        "diag_blocks": draw_diag_blocks(jax.random.fold_in(keys[8], 71), 0),
        "east_blocks": draw_east_blocks(jax.random.fold_in(keys[8], 71), 0),
        "north_blocks": draw_north_blocks(jax.random.fold_in(keys[8], 71), 0),
        "face_open": with_ends((jax.random.randint(keys[4], (NX, NY, 2), 0, 8) < 7).astype(jnp.int32), jax.random.fold_in(keys[4], 1), 0, 1),
        "modes": scatter_about(keys[5], (NX, NY, MODES, NB), (4 * NB) ** -0.5, 0.21875, ((0, 8), (1, 4)), jnp.float32),
        "aggregate": draw_aggregate(jax.random.fold_in(keys[8], 71), 0),
        "live_count": draw_live_count(jax.random.fold_in(keys[8], 71), 0),
    }


HIGH = lax.Precision.HIGHEST

def apply_operator(field, diag_blocks, east_blocks, north_blocks, open_x, open_y):
    own = jnp.einsum('xyij,xyj->xyi', diag_blocks, field, precision=HIGH)
    zero_x = jnp.zeros_like(field[:1])
    zero_y = jnp.zeros_like(field[:, :1])
    field_east = jnp.concatenate([field[1:], zero_x], 0)
    field_north = jnp.concatenate([field[:, 1:], zero_y], 1)
    ahead_x = jnp.einsum('xyij,xyj->xyi', east_blocks, field_east, precision=HIGH) * open_x[..., None]
    ahead_y = jnp.einsum('xyij,xyj->xyi', north_blocks, field_north, precision=HIGH) * open_y[..., None]
    back_x = jnp.einsum('xyij,xyi->xyj', east_blocks, field, precision=HIGH) * open_x[..., None]
    back_y = jnp.einsum('xyij,xyi->xyj', north_blocks, field, precision=HIGH) * open_y[..., None]
    back_x = jnp.concatenate([zero_x, back_x[:-1]], 0)
    back_y = jnp.concatenate([zero_y, back_y[:, :-1]], 1)
    return own + ahead_x + ahead_y + back_x + back_y

def by_device(array):
    shape = array.shape
    return array.reshape((NX // EX, EX, NY // EY, EY) + shape[2:])

def reference(rhs, diag_blocks, east_blocks, north_blocks, face_open, modes, aggregate, live_count):
    open_x = face_open[..., 0].astype(jnp.float32)
    open_y = face_open[..., 1].astype(jnp.float32)

    def operate(field):
        return apply_operator(field, diag_blocks, east_blocks, north_blocks, open_x, open_y)
    inv_diag = 1.0 / jnp.diagonal(diag_blocks, axis1=2, axis2=3)
    scaled = inv_diag * operate(rhs)
    lam = jnp.sqrt(jnp.sum(scaled * scaled) / (jnp.sum(rhs * rhs) + 1e-06))
    upper = 1.1 * lam
    lower = 0.3 * lam
    theta = 0.5 * (upper + lower)
    delta = 0.5 * (upper - lower)
    sigma = theta / delta
    rho = 1.0 / sigma
    step_dir = inv_diag * rhs / theta
    solution = step_dir
    for count in range(CHEB - 1):
        resid = rhs - operate(solution)
        rho_new = 1.0 / (2.0 * sigma - rho)
        step_dir = rho_new * rho * step_dir + 2.0 * rho_new / delta * inv_diag * resid
        solution = solution + step_dir
        rho = rho_new
    residual = rhs - operate(solution)
    onehot = jax.nn.one_hot(aggregate, AGG_DEV, dtype=jnp.float32)
    weighted = jnp.einsum('xymi,xyij->xymj', modes, diag_blocks, precision=HIGH)
    g_self = jnp.einsum('xymj,xynj->xymn', weighted, modes, precision=HIGH)
    modes_east = jnp.concatenate([modes[1:], jnp.zeros_like(modes[:1])], 0)
    modes_north = jnp.concatenate([modes[:, 1:], jnp.zeros_like(modes[:, :1])], 1)
    hot_east = jnp.concatenate([onehot[1:], jnp.zeros_like(onehot[:1])], 0)
    hot_north = jnp.concatenate([onehot[:, 1:], jnp.zeros_like(onehot[:, :1])], 1)
    weighted_x = jnp.einsum('xymi,xyij->xymj', modes, east_blocks, precision=HIGH)
    g_east = jnp.einsum('xymj,xynj->xymn', weighted_x, modes_east, precision=HIGH) * open_x[..., None, None]
    weighted_y = jnp.einsum('xymi,xyij->xymj', modes, north_blocks, precision=HIGH)
    g_north = jnp.einsum('xymj,xynj->xymn', weighted_y, modes_north, precision=HIGH) * open_y[..., None, None]
    local_x = jnp.arange(NX) % EX
    local_y = jnp.arange(NY) % EY
    inner_x = (local_x < EX - 1).astype(jnp.float32)[:, None, None]
    cross_x = (local_x == EX - 1).astype(jnp.float32)[:, None, None]
    inner_y = (local_y < EY - 1).astype(jnp.float32)[None, :, None]
    cross_y = (local_y == EY - 1).astype(jnp.float32)[None, :, None]
    form = 'gpqsa,gpqsb,gpqsmn->gqambn'
    form_t = 'gpqsa,gpqsb,gpqsnm->gqambn'
    self_part = jnp.einsum(form, by_device(onehot), by_device(onehot), by_device(g_self), precision=HIGH)
    self_part = self_part + jnp.einsum(form, by_device(onehot * inner_x), by_device(hot_east), by_device(g_east), precision=HIGH)
    self_part = self_part + jnp.einsum(form_t, by_device(hot_east * inner_x), by_device(onehot), by_device(g_east), precision=HIGH)
    self_part = self_part + jnp.einsum(form, by_device(onehot * inner_y), by_device(hot_north), by_device(g_north), precision=HIGH)
    self_part = self_part + jnp.einsum(form_t, by_device(hot_north * inner_y), by_device(onehot), by_device(g_north), precision=HIGH)
    east_part = jnp.einsum(form, by_device(onehot * cross_x), by_device(hot_east), by_device(g_east), precision=HIGH)
    north_part = jnp.einsum(form, by_device(onehot * cross_y), by_device(hot_north), by_device(g_north), precision=HIGH)
    groups = NX // EX
    members = NY // EY
    flat = (groups, members, AGG_DEV, MODES, AGG_DEV * MODES)
    rows = jnp.concatenate([self_part.reshape(flat), east_part.reshape(flat), north_part.reshape(flat)], -1)
    projected = jnp.einsum('xymi,xyi->xym', modes, residual, precision=HIGH)
    crhs = jnp.einsum('gpqsa,gpqsm->gqam', by_device(onehot), by_device(projected), precision=HIGH)
    offsets = jnp.cumsum(live_count, axis=1) - live_count
    slots = jnp.arange(CAP, dtype=jnp.int32)
    index_a = jnp.arange(AGG_DEV, dtype=jnp.int32)
    target = offsets[:, :, None] + index_a[None, None, :]
    live = index_a[None, None, :] < live_count[:, :, None]
    place = ((slots[None, None, None, :] == target[..., None]) & live[..., None]).astype(jnp.float32)
    packed_rows = jnp.einsum('gqas,gqamc->gsmc', place, rows, precision=HIGH)
    packed_rhs = jnp.einsum('gqas,gqam->gsm', place, crhs, precision=HIGH)
    coarse_rows = jnp.zeros((groups, members, CAP, MODES, COLS), jnp.float32).at[:, 0].set(packed_rows)
    coarse_rhs = jnp.zeros((groups, members, CAP, MODES), jnp.float32).at[:, 0].set(packed_rhs)
    return (solution, coarse_rows, coarse_rhs)
```

```python
import functools

import jax
import jax.numpy as jnp
from jax import lax
from jax.experimental import pallas as pl
from jax.experimental.pallas import tpu as pltpu
from jax.sharding import PartitionSpec as P

MODES = 6
CHEB = 4
AGG_DEV = 16
PASSES = CHEB + 1
F32 = jnp.float32
BF16 = jnp.bfloat16
NN = (((1,), (0,)), ((), ()))
NT = (((1,), (1,)), ((), ()))


def split(value):
    high = value.astype(BF16)
    return high, (value - high.astype(F32)).astype(BF16)


def mul(a, b, dims):
    return lax.dot_general(a, b, dims, preferred_element_type=F32)


def mul_split(a, b, dims):
    a_high, a_low = split(a)
    b_high, b_low = split(b)
    return mul(a_high, b_high, dims) + (mul(a_low, b_high, dims) + mul(a_high, b_low, dims))


def mul_left_hot(hot, b):
    b_high, b_low = split(b)
    hot = hot.astype(BF16)
    return mul(hot, b_high, NN) + mul(hot, b_low, NN)


def mul_right_hot(a, hot):
    a_high, a_low = split(a)
    hot = hot.astype(BF16)
    return mul(a_high, hot, NN) + mul(a_low, hot, NN)


def iota(shape, dim):
    return lax.broadcasted_iota(jnp.int32, shape, dim)


def kernel(
    sizes,
    rhs, diag_hbm, east_hbm, north_hbm, face, modes, aggregate, live,
    x_out, rows_out, crhs_out,
    diag, east, north, inv, field, ahead, back_x, back_y, step_ref, coef,
    wall, hot6, hot8, hot_at, wide_hot, r_diag, r_east, r_north,
    w_stage, q_stage, v_stage, y_stage,
    v_east, v_north, b_west, b_south,
    sum_own, sum_own2, sum_gy, sum_gx, gath, gath2, rows_own, crhs_own, proj,
    load_sem, halo_send, halo_recv, mode_send, mode_recv,
    gy_send, gy_recv, gx_send, gx_recv, rows_send, rows_recv, crhs_send, crhs_recv,
):
    gxs, gys, ex, ey, nb = sizes
    ne = ex * ey
    slots = ne + 16
    cap = gys * AGG_DEV
    g = lax.axis_index("gx")
    q = lax.axis_index("gy")

    loads = {}
    for i in range(ex):
        for k, (src, dst) in enumerate(((diag_hbm, diag), (east_hbm, east), (north_hbm, north))):
            loads[i, k] = pltpu.make_async_copy(src.at[i], dst.at[i], load_sem.at[i, k])
            loads[i, k].start()

    v_east[...] = jnp.zeros_like(v_east)
    v_north[...] = jnp.zeros_like(v_north)
    b_west[...] = jnp.zeros_like(b_west)
    b_south[...] = jnp.zeros_like(b_south)
    wall[ne:] = jnp.zeros((16, 8, nb), F32)
    hot6[ne:] = jnp.zeros((16, 8, 128), F32)
    v_stage[...] = jnp.zeros_like(v_stage)
    y_stage[...] = jnp.zeros_like(y_stage)

    barrier = pltpu.get_barrier_semaphore()
    for k in range(1, gys):
        pl.semaphore_signal(barrier, inc=1, device_id={"gy": lax.rem(q + k, gys)}, device_id_type=pl.DeviceIdType.MESH)
    for k in range(1, gxs):
        pl.semaphore_signal(barrier, inc=1, device_id={"gx": lax.rem(g + k, gxs)}, device_id_type=pl.DeviceIdType.MESH)

    sub = iota((8, 128), 0)
    lane = iota((8, 128), 1)
    sub3 = iota((8, 384), 0)
    lane3 = iota((8, 384), 1)

    def prepare(i, _):
        for j in range(ey):
            e = i * ey + j
            slot = aggregate[i, j]
            wall[e] = jnp.concatenate([modes[i, j], jnp.zeros((8 - MODES, nb), F32)], 0)
            hot6[e] = jnp.where((lane == MODES * slot + sub) & (sub < MODES), 1.0, 0.0)
            hot8[e] = jnp.where(lane == 8 * slot + sub, 1.0, 0.0)
            hot_at[e] = jnp.where(lane == slot, 1.0, 0.0)
            wide_hot[e] = jnp.where((lane3 == MODES * slot + sub3) & (sub3 < MODES), 1.0, 0.0)
        w_stage[i] = wall[i * ey]
        q_stage[i] = hot6[i * ey]
        return 0

    lax.fori_loop(0, ex, prepare, 0)
    field[...] = jnp.zeros_like(field)
    field[0:ex, 0:ey] = rhs[...]

    pl.semaphore_wait(barrier, gxs + gys - 2)

    def remote(src, dst, send, recv, **where):
        return pltpu.make_async_remote_copy(
            src_ref=src, dst_ref=dst, send_sem=send, recv_sem=recv,
            device_id=where, device_id_type=pl.DeviceIdType.MESH,
        )

    has_west, has_east = g > 0, g < gxs - 1
    has_south, has_north = q > 0, q < gys - 1
    west, east_g = jnp.maximum(g - 1, 0), jnp.minimum(g + 1, gxs - 1)
    south, north_q = jnp.maximum(q - 1, 0), jnp.minimum(q + 1, gys - 1)

    mode_copies = (
        (has_west, has_east, remote(wall.at[pl.ds(0, ey)], wall.at[pl.ds(ne, ey)], mode_send.at[0], mode_recv.at[0], gx=west)),
        (has_west, has_east, remote(hot6.at[pl.ds(0, ey)], hot6.at[pl.ds(ne, ey)], mode_send.at[1], mode_recv.at[1], gx=west)),
        (has_south, has_north, remote(w_stage, wall.at[pl.ds(ne + 8, ex)], mode_send.at[2], mode_recv.at[2], gy=south)),
        (has_south, has_north, remote(q_stage, hot6.at[pl.ds(ne + 8, ex)], mode_send.at[3], mode_recv.at[3], gy=south)),
    )
    for sends, _, copy in mode_copies:
        pl.when(sends)(copy.start)

    same = iota((nb, nb), 0) == iota((nb, nb), 1)

    def coarse_row(i, _):
        for k, (src, dst) in enumerate(((diag_hbm, diag), (east_hbm, east), (north_hbm, north))):
            pltpu.make_async_copy(src.at[i], dst.at[i], load_sem.at[i, k]).wait()
        for j in range(ey):
            e = i * ey + j
            main = jnp.sum(jnp.where(same, diag[i, j], 0.0), axis=0, keepdims=True)
            inv[i, pl.ds(j, 1), :] = 1.0 / main
            w = wall[e]
            w_high = w.astype(BF16).astype(F32)
            both = jnp.concatenate([w_high, w - w_high], 0).astype(BF16)
            for block, result, scale in (
                (diag, r_diag, None),
                (east, r_east, face[i, j, 0].astype(F32)),
                (north, r_north, face[i, j, 1].astype(F32)),
            ):
                high, low = split(block[i, j])
                product = mul(both, high, NN) + mul(both, low, NN)
                product = product[:8] + product[8:]
                result[e] = product if scale is None else product * scale
        return 0

    lax.fori_loop(0, ex, coarse_row, 0)

    for sends, receives, copy in mode_copies:
        pl.when(receives)(copy.wait_recv)
        pl.when(sends)(copy.wait_send)

    shape = (ne * 8, slots * 8)
    row_e = lax.shift_right_logical(iota(shape, 0), 3)
    col_e = lax.shift_right_logical(iota(shape, 1), 3)
    row_j = row_e & (ey - 1)
    row_i = lax.shift_right_logical(row_e, ey.bit_length() - 1)
    w_all = wall[...].reshape(slots * 8, nb)
    on_main = mul_split(r_diag[...].reshape(ne * 8, nb), w_all, NT)
    on_east = mul_split(r_east[...].reshape(ne * 8, nb), w_all, NT)
    on_north = mul_split(r_north[...].reshape(ne * 8, nb), w_all, NT)
    next_y = jnp.where(row_j < ey - 1, row_e + 1, ne + 8 + row_i)
    coupling = jnp.where(col_e == row_e + ey, on_east, 0.0) + jnp.where(col_e == next_y, on_north, 0.0)
    main_part = jnp.where(col_e == row_e, on_main, 0.0) + coupling
    halo_x = jnp.concatenate([hot6[ne : ne + 8].reshape(64, 128), jnp.zeros((64, 256), F32)], 1)
    halo_y = jnp.concatenate([hot6[ne + 8 :].reshape(64, 128), jnp.zeros((64, 256), F32)], 1)
    wide_hot[ne : ne + 8] = pltpu.roll(halo_x, 96, 1).reshape(8, 8, 384)
    wide_hot[ne + 8 :] = pltpu.roll(halo_y, 192, 1).reshape(8, 8, 384)
    wide = wide_hot[...].reshape(slots * 8, 384)
    spread = mul_right_hot(main_part, wide)
    spread = spread + mul_right_hot(coupling[:, : ne * 8].T, wide[: ne * 8])
    hot8_t = hot8[...].reshape(ne * 8, 128).T
    rows = mul_left_hot(hot8_t, spread)
    count = live[0, 0].astype(F32)
    rows_own[...] = jnp.where(iota(rows.shape, 1) >= 288, count, rows)

    rows_copy = remote(rows_own, gath.at[q], rows_send, rows_recv.at[q], gy=0 * q)
    pl.when(q > 0)(rows_copy.start)

    sum_copies_gy = [
        remote(sum_own, sum_gy.at[k - 1], gy_send.at[k - 1], gy_recv.at[k - 1], gy=lax.rem(q + k, gys))
        for k in range(1, gys)
    ]
    sum_copies_gx = [
        remote(sum_own2, sum_gx.at[k - 1], gx_send.at[k - 1], gx_recv.at[k - 1], gx=lax.rem(g + k, gxs))
        for k in range(1, gxs)
    ]

    def backs(i, j):
        own = field[i, pl.ds(j, 1), :]
        column = jnp.broadcast_to(own, (128, nb)).T
        short = column[:, : nb - 128]
        ox = face[i, j, 0].astype(F32)
        oy = face[i, j, 1].astype(F32)
        for block, result, at, scale in (
            (east, back_x, (i + 1, pl.ds(j, 1)), ox),
            (north, back_y, (i, pl.ds(j + 1, 1)), oy),
        ):
            result[at + (slice(0, 128),)] = scale * jnp.sum(block[i, j, :, 0:128] * column, axis=0, keepdims=True)
            result[at + (slice(128, nb),)] = scale * jnp.sum(block[i, j, :, 128:nb] * short, axis=0, keepdims=True)

    def aheads(i, j):
        ox = face[i, j, 0].astype(F32)
        oy = face[i, j, 1].astype(F32)
        own = field[i, pl.ds(j, 1), :]
        ve = field[i + 1, pl.ds(j, 1), :] * ox
        vn = field[i, pl.ds(j + 1, 1), :] * oy

        def part(s, t):
            cut = slice(s, t)
            return (
                diag[i, j, :, cut] * own[:, cut]
                + east[i, j, :, cut] * ve[:, cut]
                + north[i, j, :, cut] * vn[:, cut]
            )

        rest = jnp.concatenate([part(128, nb), jnp.zeros((nb, 256 - nb), F32)], 1)
        total = part(0, 128) + rest
        ahead[i, pl.ds(j, 1), :] = jnp.sum(total.T, axis=0, keepdims=True)

    last_x, last_y = ex - 1, ey - 1

    def one_pass(k, _):
        for i in range(ex):
            v_stage[pl.ds(i, 1), :] = field[i, 0:1, :]
        go_w = remote(field.at[0, pl.ds(0, ey)], v_east.at[k], halo_send.at[k, 0], halo_recv.at[k, 0], gx=west)
        go_s = remote(v_stage, v_north.at[k], halo_send.at[k, 1], halo_recv.at[k, 1], gy=south)
        go_e = remote(back_x.at[ex], b_west.at[k], halo_send.at[k, 2], halo_recv.at[k, 2], gx=east_g)
        go_n = remote(y_stage, b_south.at[k], halo_send.at[k, 3], halo_recv.at[k, 3], gy=north_q)
        pl.when(has_west)(go_w.start)
        pl.when(has_south)(go_s.start)
        for j in range(ey):
            backs(last_x, j)
        pl.when(has_east)(go_e.start)
        for i in range(last_x):
            backs(i, last_y)
        for i in range(ex):
            y_stage[pl.ds(i, 1), :] = back_y[i, ey : ey + 1, :]
        pl.when(has_north)(go_n.start)

        def inner(i, _):
            for j in range(last_y):
                backs(i, j)
                aheads(i, j)
            return 0

        lax.fori_loop(0, last_x, inner, 0)

        @pl.when(k == 1)
        def _():
            total = sum_own[...]
            for n, copy in enumerate(sum_copies_gy):
                copy.wait()
                total = total + sum_gy[n]
            sum_own2[...] = total
            for copy in sum_copies_gx:
                copy.start()

        pl.when(has_east)(go_w.wait_recv)
        pl.when(has_north)(go_s.wait_recv)
        field[ex, 0:ey] = v_east[k]
        for i in range(ex):
            field[i, ey : ey + 1, :] = v_north[k, i : i + 1, :]
        for j in range(ey):
            aheads(last_x, j)
        for i in range(last_x):
            aheads(i, last_y)
        pl.when(has_west)(go_e.wait_recv)
        pl.when(has_south)(go_n.wait_recv)
        back_x[0] = b_west[k]
        for i in range(ex):
            back_y[i, 0:1, :] = b_south[k, i : i + 1, :]
        pl.when(has_west)(go_w.wait_send)
        pl.when(has_south)(go_s.wait_send)
        pl.when(has_east)(go_e.wait_send)
        pl.when(has_north)(go_n.wait_send)
        applied = ahead[...] + back_x[0:ex] + back_y[:, 0:ey]
        ahead[...] = applied

        @pl.when(k == 0)
        def _():
            scaled = inv[...] * applied
            base = rhs[...]

            def fold(value):
                value = jnp.sum(value * value, axis=0)
                rest = jnp.concatenate([value[:, 128:], jnp.zeros((ey, 256 - nb), F32)], 1)
                return value[:, :128] + rest

            sum_own[0] = fold(scaled)
            sum_own[1] = fold(base)
            for copy in sum_copies_gy:
                copy.start()
            field[0:ex, 0:ey] = inv[...] * base

        @pl.when(k == 1)
        def _():
            total = sum_own2[...]
            for n, copy in enumerate(sum_copies_gx):
                copy.wait()
                total = total + sum_gx[n]
            top = jnp.sum(jnp.sum(total[0], axis=1, keepdims=True), axis=0, keepdims=True)
            bottom = jnp.sum(jnp.sum(total[1], axis=1, keepdims=True), axis=0, keepdims=True)
            lam = jnp.broadcast_to(jnp.sqrt(top / (bottom + 1e-06)), (1, nb))
            upper = 1.1 * lam
            lower = 0.3 * lam
            theta = 0.5 * (upper + lower)
            delta = 0.5 * (upper - lower)
            sigma = theta / delta
            coef[0:1] = sigma
            coef[1:2] = delta
            coef[2:3] = 1.0 / sigma
            start = field[0:ex, 0:ey] / theta.reshape(1, 1, nb)
            step_ref[...] = start
            field[0:ex, 0:ey] = start
            ahead[...] = ahead[...] / theta.reshape(1, 1, nb)

        @pl.when((k >= 1) & (k < PASSES - 1))
        def _():
            resid = rhs[...] - ahead[...]
            sigma, delta, rho = coef[0:1], coef[1:2], coef[2:3]
            rho_new = 1.0 / (2.0 * sigma - rho)
            keep = (rho_new * rho).reshape(1, 1, nb)
            gain = (2.0 * rho_new / delta).reshape(1, 1, nb)
            step = keep * step_ref[...] + gain * inv[...] * resid
            step_ref[...] = step
            field[0:ex, 0:ey] = field[0:ex, 0:ey] + step
            coef[2:3] = rho_new

        return 0

    lax.fori_loop(0, PASSES, one_pass, 0)
    x_out[...] = field[0:ex, 0:ey]
    ahead[...] = rhs[...] - ahead[...]

    def project(i, _):
        for j in range(ey):
            e = i * ey + j
            dots = jnp.sum(wall[e] * ahead[i, pl.ds(j, 1), :], axis=1, keepdims=True)
            proj[e] = jnp.where(lane == sub, dots, 0.0)
        return 0

    lax.fori_loop(0, ex, project, 0)
    at_t = hot_at[...].reshape(ne * 8, 128).T[:AGG_DEV]
    crhs_own[...] = mul_left_hot(at_t, proj[...].reshape(ne * 8, 128))
    crhs_copy = remote(crhs_own, gath2.at[q], crhs_send, crhs_recv.at[q], gy=0 * q)

    @pl.when(q > 0)
    def _():
        crhs_copy.start()
        rows_out[...] = jnp.zeros_like(rows_out)
        crhs_out[...] = jnp.zeros_like(crhs_out)
        rows_copy.wait_send()
        crhs_copy.wait_send()

    @pl.when(q == 0)
    def _():
        gath[0] = rows_own[...]
        gath2[0] = crhs_own[...]
        for n in range(1, gys):
            remote(rows_own, gath.at[n], rows_send, rows_recv.at[n], gy=0 * q).wait_recv()
        p_shape = (cap * 8, AGG_DEV * 8)
        p_row = iota(p_shape, 0)
        p_col = iota(p_shape, 1)
        shift = (lax.shift_right_logical(p_row, 3) - lax.shift_right_logical(p_col, 3)).astype(F32)
        a_index = lax.shift_right_logical(p_col, 3).astype(F32)
        same_m = (p_row & 7) == (p_col & 7)
        s_shape = (cap, AGG_DEV)
        s_shift = (iota(s_shape, 0) - iota(s_shape, 1)).astype(F32)
        s_index = iota(s_shape, 1).astype(F32)
        offset = jnp.zeros((1, 1), F32)
        packed = jnp.zeros((cap * 8, 384), F32)
        places = []
        for n in range(gys):
            number = gath[n, 0:1, 288:289]
            hot = jnp.where((shift == offset) & same_m & (a_index < number), 1.0, 0.0)
            packed = packed + mul_left_hot(hot, gath[n])
            places.append(jnp.where((s_shift == offset) & (s_index < number), 1.0, 0.0))
            offset = offset + number
        rows_out[...] = packed.reshape(cap, 8, 384)[:, :MODES, :288]
        for n in range(1, gys):
            remote(crhs_own, gath2.at[n], crhs_send, crhs_recv.at[n], gy=0 * q).wait_recv()
        packed_rhs = jnp.zeros((cap, 128), F32)
        for n in range(gys):
            packed_rhs = packed_rhs + mul_left_hot(places[n], gath2[n])
        crhs_out[...] = packed_rhs[:, :MODES]


def solution(mesh):
    gxs, gys = mesh.shape["gx"], mesh.shape["gy"]

    def per_device(rhs, diag_blocks, east_blocks, north_blocks, face_open, modes, aggregate, live_count):
        ex, ey, nb = rhs.shape
        ne = ex * ey
        cap = gys * AGG_DEV
        block = (ex, ey, nb, nb)
        dma = pltpu.SemaphoreType.DMA

        def vmem(*shape):
            return pltpu.VMEM(shape, F32)

        x, rows, crhs = pl.pallas_call(
            functools.partial(kernel, (gxs, gys, ex, ey, nb)),
            out_shape=(
                jax.ShapeDtypeStruct((ex, ey, nb), F32),
                jax.ShapeDtypeStruct((cap, MODES, 288), F32),
                jax.ShapeDtypeStruct((cap, MODES), F32),
            ),
            in_specs=[
                pl.BlockSpec(memory_space=pltpu.VMEM),
                pl.BlockSpec(memory_space=pl.ANY),
                pl.BlockSpec(memory_space=pl.ANY),
                pl.BlockSpec(memory_space=pl.ANY),
                pl.BlockSpec(memory_space=pltpu.SMEM),
                pl.BlockSpec(memory_space=pltpu.VMEM),
                pl.BlockSpec(memory_space=pltpu.SMEM),
                pl.BlockSpec(memory_space=pltpu.SMEM),
            ],
            out_specs=[pl.BlockSpec(memory_space=pltpu.VMEM)] * 3,
            scratch_shapes=[
                vmem(*block), vmem(*block), vmem(*block),
                vmem(ex, ey, nb), vmem(ex + 1, ey + 8, nb), vmem(ex, ey, nb),
                vmem(ex + 1, ey, nb), vmem(ex, ey + 8, nb), vmem(ex, ey, nb), vmem(8, nb),
                vmem(ne + 16, 8, nb), vmem(ne + 16, 8, 128), vmem(ne, 8, 128), vmem(ne, 8, 128),
                vmem(ne + 16, 8, 384), vmem(ne, 8, nb), vmem(ne, 8, nb), vmem(ne, 8, nb),
                vmem(ex, 8, nb), vmem(ex, 8, 128), vmem(8, nb), vmem(8, nb),
                vmem(PASSES, ey, nb), vmem(PASSES, 8, nb), vmem(PASSES, ey, nb), vmem(PASSES, 8, nb),
                vmem(2, ey, 128), vmem(2, ey, 128), vmem(gys - 1, 2, ey, 128), vmem(gxs - 1, 2, ey, 128),
                vmem(gys, 128, 384), vmem(gys, AGG_DEV, 128), vmem(128, 384), vmem(AGG_DEV, 128),
                vmem(ne, 8, 128),
                dma((ex, 3)), dma((PASSES, 4)), dma((PASSES, 4)), dma((4,)), dma((4,)),
                dma((gys - 1,)), dma((gys - 1,)), dma((gxs - 1,)), dma((gxs - 1,)),
                dma, dma((gys,)), dma, dma((gys,)),
            ],
            compiler_params=pltpu.CompilerParams(
                collective_id=0, has_side_effects=True, vmem_limit_bytes=60 << 20
            ),
        )(rhs, diag_blocks, east_blocks, north_blocks, face_open, modes, aggregate, live_count)
        return x, rows[None, None], crhs[None, None]

    in_specs = (
        P("gx", "gy", None),
        P("gx", "gy", None, None),
        P("gx", "gy", None, None),
        P("gx", "gy", None, None),
        P("gx", "gy", None),
        P("gx", "gy", None, None),
        P("gx", "gy"),
        P("gx", "gy"),
    )
    out_specs = (P("gx", "gy", None), P("gx", "gy", None, None, None), P("gx", "gy", None, None))
    return jax.shard_map(
        per_device, mesh=mesh, in_specs=in_specs, out_specs=out_specs, check_vma=False
    )
```

```python
import functools

import jax
import jax.numpy as jnp
from jax import lax
from jax.experimental import pallas as pl
from jax.experimental.pallas import tpu as pltpu
from jax.sharding import PartitionSpec as P

MODES = 6
CHEB = 4
AGG_DEV = 16
PASSES = CHEB + 1
CHUNK = 48
F32 = jnp.float32
BF16 = jnp.bfloat16
NN = (((1,), (0,)), ((), ()))
NT = (((1,), (1,)), ((), ()))


def split(value):
    high = value.astype(BF16)
    return high, (value - high.astype(F32)).astype(BF16)


def mul(a, b, dims):
    return lax.dot_general(a, b, dims, preferred_element_type=F32)


def mul_split(a, b, dims):
    a_high, a_low = split(a)
    b_high, b_low = split(b)
    return mul(a_high, b_high, dims) + (mul(a_low, b_high, dims) + mul(a_high, b_low, dims))


def mul_left_hot(hot, b):
    b_high, b_low = split(b)
    hot = hot.astype(BF16)
    return mul(hot, b_high, NN) + mul(hot, b_low, NN)


def mul_right_hot(a, hot):
    a_high, a_low = split(a)
    hot = hot.astype(BF16)
    return mul(a_high, hot, NN) + mul(a_low, hot, NN)


def iota(shape, dim):
    return lax.broadcasted_iota(jnp.int32, shape, dim)


def kernel(
    sizes,
    rhs, diag_hbm, east_hbm, north_hbm, face, modes, aggregate, live,
    x_out, gath, gath2,
    diag, east, north, pack, inv, field, main_ref, ahead, back_x, back_y, step_ref, coef,
    wall, hot6, hot8, hot_at, wide_hot, r_diag, r_east, r_north,
    w_stage, q_stage, v_stage, y_stage,
    v_east, v_north, b_west, b_south,
    sum_own, sum_own2, sum_gy, sum_gx, rows_own, crhs_own, proj,
    load_sem, halo_send, halo_recv, mode_send, mode_recv,
    gy_send, gy_recv, gx_send, gx_recv, rows_send, rows_recv, crhs_send, crhs_recv,
):
    gxs, gys, ex, ey, nb = sizes
    ne = ex * ey
    slots = ne + 16
    g = lax.axis_index("gx")
    q = lax.axis_index("gy")

    loads = {}
    for i in range(ex):
        for k, (src, dst) in enumerate(((diag_hbm, diag), (east_hbm, east), (north_hbm, north))):
            loads[i, k] = pltpu.make_async_copy(src.at[i], dst.at[i], load_sem.at[i, k])
            loads[i, k].start()

    v_east[...] = jnp.zeros_like(v_east)
    v_north[...] = jnp.zeros_like(v_north)
    b_west[...] = jnp.zeros_like(b_west)
    b_south[...] = jnp.zeros_like(b_south)
    wall[ne:] = jnp.zeros((16, 8, nb), F32)
    hot6[ne:] = jnp.zeros((16, 8, 128), F32)
    v_stage[...] = jnp.zeros_like(v_stage)
    y_stage[...] = jnp.zeros_like(y_stage)

    barrier = pltpu.get_barrier_semaphore()
    for k in range(1, gys):
        pl.semaphore_signal(barrier, inc=1, device_id={"gy": lax.rem(q + k, gys)}, device_id_type=pl.DeviceIdType.MESH)
    for k in range(1, gxs):
        pl.semaphore_signal(barrier, inc=1, device_id={"gx": lax.rem(g + k, gxs)}, device_id_type=pl.DeviceIdType.MESH)

    sub = iota((8, 128), 0)
    lane = iota((8, 128), 1)
    sub3 = iota((8, 384), 0)
    lane3 = iota((8, 384), 1)

    def prepare(i, _):
        for j in range(ey):
            e = i * ey + j
            slot = aggregate[i, j]
            wall[e, MODES:] = jnp.zeros((8 - MODES, nb), F32)
            for m in range(MODES):
                wall[e, m : m + 1, :] = modes[i, m, j : j + 1, :]
            hot6[e] = jnp.where((lane == MODES * slot + sub) & (sub < MODES), 1.0, 0.0)
            hot8[e] = jnp.where(lane == AGG_DEV * sub + slot, 1.0, 0.0)
            hot_at[e] = jnp.where(lane == slot, 1.0, 0.0)
            wide_hot[e] = jnp.where((lane3 == MODES * slot + sub3) & (sub3 < MODES), 1.0, 0.0)
        w_stage[i] = wall[i * ey]
        q_stage[i] = hot6[i * ey]
        return 0

    lax.fori_loop(0, ex, prepare, 0)
    field[...] = jnp.zeros_like(field)
    field[0:ex, 0:ey] = rhs[...]

    pl.semaphore_wait(barrier, gxs + gys - 2)

    def remote(src, dst, send, recv, **where):
        return pltpu.make_async_remote_copy(
            src_ref=src, dst_ref=dst, send_sem=send, recv_sem=recv,
            device_id=where, device_id_type=pl.DeviceIdType.MESH,
        )

    has_west, has_east = g > 0, g < gxs - 1
    has_south, has_north = q > 0, q < gys - 1
    west, east_g = jnp.maximum(g - 1, 0), jnp.minimum(g + 1, gxs - 1)
    south, north_q = jnp.maximum(q - 1, 0), jnp.minimum(q + 1, gys - 1)

    mode_copies = (
        (has_west, has_east, remote(wall.at[pl.ds(0, ey)], wall.at[pl.ds(ne, ey)], mode_send.at[0], mode_recv.at[0], gx=west)),
        (has_west, has_east, remote(hot6.at[pl.ds(0, ey)], hot6.at[pl.ds(ne, ey)], mode_send.at[1], mode_recv.at[1], gx=west)),
        (has_south, has_north, remote(w_stage, wall.at[pl.ds(ne + 8, ex)], mode_send.at[2], mode_recv.at[2], gy=south)),
        (has_south, has_north, remote(q_stage, hot6.at[pl.ds(ne + 8, ex)], mode_send.at[3], mode_recv.at[3], gy=south)),
    )
    for sends, _, copy in mode_copies:
        pl.when(sends)(copy.start)

    half = nb // 2

    def fold(value):
        return jnp.sum(value.reshape(-1, 8, 128), axis=0)

    def down(value):
        return jnp.sum(value, axis=0, keepdims=True)

    def element(i, j, local, forward):
        at = pl.ds(j, 1)
        ox = face[i, 0, j].astype(F32)
        oy = face[i, 1, j].astype(F32)
        if local:
            column = jnp.broadcast_to(field[i, at, :], (128, nb)).T
        if forward:
            ve = field[i + 1, at, :] * ox
            vn = field[i, pl.ds(j + 1, 1), :] * oy
            vb = jnp.concatenate([ve[:, 128:], vn[:, 128:]], 1)
            ve, vn = ve[:, :128], vn[:, :128]
        parts = []
        sums = [jnp.zeros((8, 128), F32)] * 5
        for c in range(0, nb, CHUNK):
            ea = east[i, j, c : c + CHUNK, 0:128]
            na = north[i, j, c : c + CHUNK, 0:128]
            pa = pack[i, j, c : c + CHUNK, :]
            if local:
                col = column[c : c + CHUNK]
                sums[0] = sums[0] + fold(ea * col)
                sums[1] = sums[1] + fold(na * col)
                sums[2] = sums[2] + fold(pa * col)
                sums[3] = sums[3] + fold(diag[i, j, c : c + CHUNK, 0:128] * col)
                if c < half:
                    other = column[c + half : c + half + CHUNK]
                    mixed = jnp.where(iota(col.shape, 1) < nb - 128, col, other)
                    sums[4] = sums[4] + fold(pack[i, j, nb + c : nb + c + CHUNK, :] * mixed)
            if forward:
                parts.append(ea * ve + na * vn + pa * vb)
        if local:
            shared = down(sums[2])
            back_x[i + 1, at, 0:128] = ox * down(sums[0])
            back_x[i + 1, at, 128:nb] = ox * shared[:, :64]
            back_y[i, pl.ds(j + 1, 1), 0:128] = oy * down(sums[1])
            back_y[i, pl.ds(j + 1, 1), 128:nb] = oy * shared[:, 64:]
            tail = down(sums[4])
            main_ref[i, at, 0:128] = down(sums[3])
            main_ref[i, at, 128:nb] = tail[:, :64] + tail[:, 64:]
        if forward:
            ahead[i, at, :] = down(jnp.concatenate(parts, 0).T)

    last_x, last_y = ex - 1, ey - 1

    def halo_copies(k):
        return (
            remote(field.at[0, pl.ds(0, ey)], v_east.at[k], halo_send.at[k, 0], halo_recv.at[k, 0], gx=west),
            remote(v_stage, v_north.at[k], halo_send.at[k, 1], halo_recv.at[k, 1], gy=south),
            remote(back_x.at[ex], b_west.at[k], halo_send.at[k, 2], halo_recv.at[k, 2], gx=east_g),
            remote(y_stage, b_south.at[k], halo_send.at[k, 3], halo_recv.at[k, 3], gy=north_q),
        )

    def send_rims(go_w, go_s):
        for i in range(ex):
            v_stage[pl.ds(i, 1), :] = field[i, 0:1, :]
        pl.when(has_west)(go_w.start)
        pl.when(has_south)(go_s.start)

    def take_rims(k, go_w, go_s):
        pl.when(has_east)(go_w.wait_recv)
        pl.when(has_north)(go_s.wait_recv)
        field[ex, 0:ey] = v_east[k]
        for i in range(ex):
            field[i, ey : ey + 1, :] = v_north[k, i : i + 1, :]

    def send_north(go_n):
        for i in range(ex):
            y_stage[pl.ds(i, 1), :] = back_y[i, ey : ey + 1, :]
        pl.when(has_north)(go_n.start)

    def finish(k, copies):
        go_w, go_s, go_e, go_n = copies
        pl.when(has_west)(go_e.wait_recv)
        pl.when(has_south)(go_n.wait_recv)
        back_x[0] = b_west[k]
        for i in range(ex):
            back_y[i, 0:1, :] = b_south[k, i : i + 1, :]
        pl.when(has_west)(go_w.wait_send)
        pl.when(has_south)(go_s.wait_send)
        pl.when(has_east)(go_e.wait_send)
        pl.when(has_north)(go_n.wait_send)
        applied = main_ref[...] + ahead[...] + back_x[0:ex] + back_y[:, 0:ey]
        ahead[...] = applied
        return applied

    first = halo_copies(0)
    send_rims(first[0], first[1])
    take_rims(0, first[0], first[1])

    same = iota((nb, nb), 0) == iota((nb, nb), 1)

    def coarse_row(i, _):
        for k, (src, dst) in enumerate(((diag_hbm, diag), (east_hbm, east), (north_hbm, north))):
            pltpu.make_async_copy(src.at[i], dst.at[i], load_sem.at[i, k]).wait()
        for j in range(ey):
            e = i * ey + j
            main = jnp.sum(jnp.where(same, diag[i, j], 0.0), axis=0, keepdims=True)
            inv[i, pl.ds(j, 1), :] = 1.0 / main
            w = wall[e]
            w_high = w.astype(BF16).astype(F32)
            both = jnp.concatenate([w_high, w - w_high], 0).astype(BF16)
            for block, result, scale in (
                (diag, r_diag, None),
                (east, r_east, face[i, 0, j].astype(F32)),
                (north, r_north, face[i, 1, j].astype(F32)),
            ):
                high, low = split(block[i, j])
                product = mul(both, high, NN) + mul(both, low, NN)
                product = product[:8] + product[8:]
                result[e] = product if scale is None else product * scale
            pack[i, j, 0:nb, :] = jnp.concatenate([east[i, j, :, 128:nb], north[i, j, :, 128:nb]], 1)
            pack[i, j, nb:, :] = jnp.concatenate([diag[i, j, 0:half, 128:nb], diag[i, j, half:nb, 128:nb]], 1)
            element(i, j, True, True)
        return 0

    lax.fori_loop(0, ex, coarse_row, 0)
    pl.when(has_east)(first[2].start)
    send_north(first[3])

    for sends, receives, copy in mode_copies:
        pl.when(receives)(copy.wait_recv)
        pl.when(sends)(copy.wait_send)

    shape = (ne * 8, slots * 8)
    row_e = lax.shift_right_logical(iota(shape, 0), 3)
    col_e = lax.shift_right_logical(iota(shape, 1), 3)
    row_j = row_e & (ey - 1)
    row_i = lax.shift_right_logical(row_e, ey.bit_length() - 1)
    w_all = wall[...].reshape(slots * 8, nb)
    on_main = mul_split(r_diag[...].reshape(ne * 8, nb), w_all, NT)
    on_east = mul_split(r_east[...].reshape(ne * 8, nb), w_all, NT)
    on_north = mul_split(r_north[...].reshape(ne * 8, nb), w_all, NT)
    next_y = jnp.where(row_j < ey - 1, row_e + 1, ne + 8 + row_i)
    coupling = jnp.where(col_e == row_e + ey, on_east, 0.0) + jnp.where(col_e == next_y, on_north, 0.0)
    main_part = jnp.where(col_e == row_e, on_main, 0.0) + coupling
    halo_x = jnp.concatenate([hot6[ne : ne + 8].reshape(64, 128), jnp.zeros((64, 256), F32)], 1)
    halo_y = jnp.concatenate([hot6[ne + 8 :].reshape(64, 128), jnp.zeros((64, 256), F32)], 1)
    wide_hot[ne : ne + 8] = pltpu.roll(halo_x, 96, 1).reshape(8, 8, 384)
    wide_hot[ne + 8 :] = pltpu.roll(halo_y, 192, 1).reshape(8, 8, 384)
    wide = wide_hot[...].reshape(slots * 8, 384)
    spread = mul_right_hot(main_part, wide)
    spread = spread + mul_right_hot(coupling[:, : ne * 8].T, wide[: ne * 8])
    hot8_t = hot8[...].reshape(ne * 8, 128).T
    rows = mul_left_hot(hot8_t, spread)
    count = live[0, 0].astype(F32)
    rows_own[...] = jnp.where(iota(rows.shape, 1) >= 288, count, rows)

    rows_copy = remote(rows_own, gath.at[q], rows_send, rows_recv.at[q], gy=0 * q)
    pl.when(q > 0)(rows_copy.start)

    sum_copies_gy = [
        remote(sum_own, sum_gy.at[k - 1], gy_send.at[k - 1], gy_recv.at[k - 1], gy=lax.rem(q + k, gys))
        for k in range(1, gys)
    ]
    sum_copies_gx = [
        remote(sum_own2, sum_gx.at[k - 1], gx_send.at[k - 1], gx_recv.at[k - 1], gx=lax.rem(g + k, gxs))
        for k in range(1, gxs)
    ]

    applied = finish(0, first)
    scaled = inv[...] * applied
    base = rhs[...]

    def squares(value):
        value = jnp.sum(value * value, axis=0)
        rest = jnp.concatenate([value[:, 128:], jnp.zeros((ey, 256 - nb), F32)], 1)
        return value[:, :128] + rest

    sum_own[0] = squares(scaled)
    sum_own[1] = squares(base)
    for copy in sum_copies_gy:
        copy.start()
    field[0:ex, 0:ey] = inv[...] * base

    def one_pass(k, _):
        copies = halo_copies(k)
        send_rims(copies[0], copies[1])
        for j in range(ey):
            element(last_x, j, True, False)
        pl.when(has_east)(copies[2].start)
        for i in range(last_x):
            element(i, last_y, True, False)
        send_north(copies[3])

        def inner(i, _):
            for j in range(last_y):
                element(i, j, True, True)
            return 0

        lax.fori_loop(0, last_x, inner, 0)

        @pl.when(k == 1)
        def _():
            total = sum_own[...]
            for n, copy in enumerate(sum_copies_gy):
                copy.wait()
                total = total + sum_gy[n]
            sum_own2[...] = total
            for copy in sum_copies_gx:
                copy.start()

        take_rims(k, copies[0], copies[1])
        for j in range(ey):
            element(last_x, j, False, True)
        for i in range(last_x):
            element(i, last_y, False, True)
        finish(k, copies)

        @pl.when(k == 1)
        def _():
            total = sum_own2[...]
            for n, copy in enumerate(sum_copies_gx):
                copy.wait()
                total = total + sum_gx[n]
            top = jnp.sum(jnp.sum(total[0], axis=1, keepdims=True), axis=0, keepdims=True)
            bottom = jnp.sum(jnp.sum(total[1], axis=1, keepdims=True), axis=0, keepdims=True)
            lam = jnp.broadcast_to(jnp.sqrt(top / (bottom + 1e-06)), (1, nb))
            upper = 1.1 * lam
            lower = 0.3 * lam
            theta = 0.5 * (upper + lower)
            delta = 0.5 * (upper - lower)
            sigma = theta / delta
            coef[0:1] = sigma
            coef[1:2] = delta
            coef[2:3] = 1.0 / sigma
            start = field[0:ex, 0:ey] / theta.reshape(1, 1, nb)
            step_ref[...] = start
            field[0:ex, 0:ey] = start
            ahead[...] = ahead[...] / theta.reshape(1, 1, nb)

        @pl.when((k >= 1) & (k < PASSES - 1))
        def _():
            resid = rhs[...] - ahead[...]
            sigma, delta, rho = coef[0:1], coef[1:2], coef[2:3]
            rho_new = 1.0 / (2.0 * sigma - rho)
            keep = (rho_new * rho).reshape(1, 1, nb)
            gain = (2.0 * rho_new / delta).reshape(1, 1, nb)
            step = keep * step_ref[...] + gain * inv[...] * resid
            step_ref[...] = step
            field[0:ex, 0:ey] = field[0:ex, 0:ey] + step
            coef[2:3] = rho_new

        return 0

    lax.fori_loop(1, PASSES, one_pass, 0)
    x_out[...] = field[0:ex, 0:ey]
    ahead[...] = rhs[...] - ahead[...]

    def project(i, _):
        for j in range(ey):
            e = i * ey + j
            dots = jnp.sum(wall[e] * ahead[i, pl.ds(j, 1), :], axis=1, keepdims=True)
            proj[e] = jnp.where(lane == sub, dots, 0.0)
        return 0

    lax.fori_loop(0, ex, project, 0)
    at_t = hot_at[...].reshape(ne * 8, 128).T[:AGG_DEV]
    crhs_own[...] = mul_left_hot(at_t, proj[...].reshape(ne * 8, 128))
    crhs_copy = remote(crhs_own, gath2.at[q], crhs_send, crhs_recv.at[q], gy=0 * q)

    @pl.when(q > 0)
    def _():
        crhs_copy.start()
        rows_copy.wait_send()
        crhs_copy.wait_send()

    @pl.when(q == 0)
    def _():
        gath[0] = rows_own[...]
        gath2[0] = crhs_own[...]
        for n in range(1, gys):
            remote(rows_own, gath.at[n], rows_send, rows_recv.at[n], gy=0 * q).wait_recv()
            remote(crhs_own, gath2.at[n], crhs_send, crhs_recv.at[n], gy=0 * q).wait_recv()


def packing(gys, x_in, gath, gath2, x_out, rows_out, crhs_out):
    cap = gys * AGG_DEV
    q = lax.axis_index("gy")
    x_out[...] = x_in[...]

    @pl.when(q > 0)
    def _():
        rows_out[...] = jnp.zeros_like(rows_out)
        crhs_out[...] = jnp.zeros_like(crhs_out)

    @pl.when(q == 0)
    def _():
        slot = iota((cap, cap), 0).astype(F32)
        source = iota((cap, cap), 1)
        owner = lax.shift_right_logical(source, AGG_DEV.bit_length() - 1)
        index = (source & (AGG_DEV - 1)).astype(F32)
        offset = jnp.zeros((1, 1), F32)
        hot = jnp.zeros((cap, cap), F32)
        for n in range(gys):
            number = gath[n, 0:1, 288:289]
            hit = (owner == n) & (slot == index + offset) & (index < number)
            hot = jnp.where(hit, 1.0, hot)
            offset = offset + number
        for m in range(MODES):
            stacked = jnp.concatenate([gath[n, m * AGG_DEV : (m + 1) * AGG_DEV, :] for n in range(gys)], 0)
            rows_out[m] = mul_left_hot(hot, stacked)[:, :288]
        packed = mul_left_hot(hot, gath2[...].reshape(cap, 128)).T
        for m in range(MODES):
            crhs_out[m] = packed[m : m + 1]


def solution(mesh):
    gxs, gys = mesh.shape["gx"], mesh.shape["gy"]

    def per_device(rhs, diag_blocks, east_blocks, north_blocks, face_open, modes, aggregate, live_count):
        ex, ey, nb = rhs.shape
        ne = ex * ey
        cap = gys * AGG_DEV
        block = (ex, ey, nb, nb)
        dma = pltpu.SemaphoreType.DMA

        def vmem(*shape):
            return pltpu.VMEM(shape, F32)

        x, gathered, gathered_rhs = pl.pallas_call(
            functools.partial(kernel, (gxs, gys, ex, ey, nb)),
            out_shape=(
                jax.ShapeDtypeStruct((ex, ey, nb), F32),
                jax.ShapeDtypeStruct((gys, 128, 384), F32),
                jax.ShapeDtypeStruct((gys, AGG_DEV, 128), F32),
            ),
            in_specs=[
                pl.BlockSpec(memory_space=pltpu.VMEM),
                pl.BlockSpec(memory_space=pl.ANY),
                pl.BlockSpec(memory_space=pl.ANY),
                pl.BlockSpec(memory_space=pl.ANY),
                pl.BlockSpec(memory_space=pltpu.SMEM),
                pl.BlockSpec(memory_space=pltpu.VMEM),
                pl.BlockSpec(memory_space=pltpu.SMEM),
                pl.BlockSpec(memory_space=pltpu.SMEM),
            ],
            out_specs=[pl.BlockSpec(memory_space=pltpu.VMEM)] * 3,
            scratch_shapes=[
                vmem(*block), vmem(*block), vmem(*block), vmem(ex, ey, nb + nb // 2, 128),
                vmem(ex, ey, nb), vmem(ex + 1, ey + 8, nb), vmem(ex, ey, nb), vmem(ex, ey, nb),
                vmem(ex + 1, ey, nb), vmem(ex, ey + 8, nb), vmem(ex, ey, nb), vmem(8, nb),
                vmem(ne + 16, 8, nb), vmem(ne + 16, 8, 128), vmem(ne, 8, 128), vmem(ne, 8, 128),
                vmem(ne + 16, 8, 384), vmem(ne, 8, nb), vmem(ne, 8, nb), vmem(ne, 8, nb),
                vmem(ex, 8, nb), vmem(ex, 8, 128), vmem(8, nb), vmem(8, nb),
                vmem(PASSES, ey, nb), vmem(PASSES, 8, nb), vmem(PASSES, ey, nb), vmem(PASSES, 8, nb),
                vmem(2, ey, 128), vmem(2, ey, 128), vmem(gys - 1, 2, ey, 128), vmem(gxs - 1, 2, ey, 128),
                vmem(128, 384), vmem(AGG_DEV, 128),
                vmem(ne, 8, 128),
                dma((ex, 3)), dma((PASSES, 4)), dma((PASSES, 4)), dma((4,)), dma((4,)),
                dma((gys - 1,)), dma((gys - 1,)), dma((gxs - 1,)), dma((gxs - 1,)),
                dma, dma((gys,)), dma, dma((gys,)),
            ],
            compiler_params=pltpu.CompilerParams(
                collective_id=0, has_side_effects=True, vmem_limit_bytes=60 << 20
            ),
        )(
            rhs, diag_blocks, east_blocks, north_blocks,
            jnp.transpose(face_open, (0, 2, 1)), jnp.transpose(modes, (0, 2, 1, 3)), aggregate, live_count,
        )
        x, rows, crhs = pl.pallas_call(
            functools.partial(packing, gys),
            out_shape=(
                jax.ShapeDtypeStruct((ex, ey, nb), F32),
                jax.ShapeDtypeStruct((MODES, cap, 288), F32),
                jax.ShapeDtypeStruct((MODES, 1, cap), F32),
            ),
            in_specs=[pl.BlockSpec(memory_space=pltpu.VMEM)] * 3,
            out_specs=[pl.BlockSpec(memory_space=pltpu.VMEM)] * 3,
        )(x, gathered, gathered_rhs)
        rows = jnp.transpose(rows, (1, 0, 2))
        return x, rows[None, None], jnp.transpose(crhs[None], (0, 2, 3, 1))

    in_specs = (
        P("gx", "gy", None),
        P("gx", "gy", None, None),
        P("gx", "gy", None, None),
        P("gx", "gy", None, None),
        P("gx", "gy", None),
        P("gx", "gy", None, None),
        P("gx", "gy"),
        P("gx", "gy"),
    )
    out_specs = (P("gx", "gy", None), P("gx", "gy", None, None, None), P("gx", "gy", None, None))
    return jax.shard_map(
        per_device, mesh=mesh, in_specs=in_specs, out_specs=out_specs, check_vma=False
    )
```
